256 devices in a mesh: feed: 4 (over z_lo, core), chan: 64 (over x, y, z_hi).
Axes of the slice: x: 4, y: 4, z: 8 (z_hi: 4, z_lo: 2; z = z_hi * 2 + z_lo), core: 2. Of those that a mesh axis runs over, the one named last changes fastest.
Arguments:
- voltages: bfloat16 [4, 2, 8192, 40, 512], P('feed', None, 'chan'), may hold values from -6 to 6
- fine_delays: int32 [32, 8192], replicated, may hold values from 0 to 8, as said below
- coarse_delays: int32 [1024, 64], replicated, may hold values from 0 to 16, as said below
Outputs:
- candidates: float32 [4, 512, 1024], P(None, ('feed', 'chan'))
The draws below stay inside these ranges and needn't reach their ends.
Inputs may be any that keep to these rules, and one draw needn't show every extreme that they name: `fine_delays`: every row reaches 8. `coarse_delays`: every row reaches 16.
All inputs are finite; a program needn't handle non-finite values.
Results may differ from the reference program's by a relative error of at most 0.0003.
Values sent between devices are 32-bit elements; how exact they have to be, the bound alone decides.
A program may use at most 128 MiB of HBM per device.

```python
import jax
import jax.numpy as jnp
from jax import lax

BEAMS = 512
CH_DEV = 128
NDM = 1024
NG = 32
FINE_MAX = 8
COARSE_MAX = 16
NWID = 4
TS = 40
CHANNELS = 8192
SUBBANDS = 64
N_FEED = 4


def draw_fine_delays(key, part):
    key = jax.random.fold_in(key, 11)
    first, second = jax.random.split(key)
    values = jax.random.randint(first, (NG, CHANNELS), 0, FINE_MAX + 1)
    places = jax.random.randint(second, (NG, 1), 0, CHANNELS)
    column = jnp.arange(CHANNELS, dtype=jnp.int32)[None, :]
    return jnp.where(column == places, FINE_MAX, values).astype(jnp.int32)


def draw_coarse_delays(key, part):
    key = jax.random.fold_in(key, 23)
    first, second = jax.random.split(key)
    values = jax.random.randint(first, (NDM, SUBBANDS), 0, COARSE_MAX + 1)
    places = jax.random.randint(second, (NDM, 1), 0, SUBBANDS)
    column = jnp.arange(SUBBANDS, dtype=jnp.int32)[None, :]
    return jnp.where(column == places, COARSE_MAX, values).astype(jnp.int32)


def block_scale(rng, shape, shards, least, high):
    def one(dim, shards_of):
        draws = jax.random.uniform(jax.random.fold_in(jax.random.fold_in(rng, 6), dim), (shards_of,), jnp.float32, least / len(shards), high / len(shards))
        return jnp.repeat(jnp.exp(draws), shape[dim] // shards_of).reshape((-1,) + (1,) * (len(shape) - dim - 1))

    level = one(*shards[0])
    for cut in shards[1:]:
        level = level * one(*cut)
    return level


def scatter_about(rng, extent, scale, bound, cuts=(), kind=jnp.bfloat16):
    level = block_scale(rng, extent, cuts, -0.22, 0.18) if cuts else 1.0
    values = jax.random.normal(rng, extent, jnp.float32) * scale * level
    return jnp.minimum(jnp.maximum(values, -bound), bound).astype(kind)


def setup_inputs(seed: int = 0) -> dict:
    key_list = jax.random.split(jax.random.key(seed), 4)
    voltages = scatter_about(key_list[0], (N_FEED, 2, CHANNELS, TS, BEAMS), 1.0, 6.0, ((0, 4), (2, 64)))
    fine_delays = draw_fine_delays(jax.random.fold_in(key_list[3], 71), 0)
    coarse_delays = draw_coarse_delays(jax.random.fold_in(key_list[3], 71), 0)
    return {"voltages": voltages, "fine_delays": fine_delays, "coarse_delays": coarse_delays}


epsilon = 1e-06

def boxcar_search(series, total_channels):
    results = []
    box = series
    width = 1
    for level in range(NWID):
        results.append(lax.optimization_barrier(jnp.max(box, axis=1)) / jnp.sqrt(jnp.float32(width * total_channels)))
        if level + 1 < NWID:
            box = box[:, :-width] + box[:, width:]
            width = width * 2
    return jnp.stack(results)

def reference(voltages, fine_delays, coarse_delays):
    span = TS - FINE_MAX
    length = span - COARSE_MAX
    per_group = NDM // NG

    def one_band(index):
        start = (index * CH_DEV).astype(jnp.int32)
        block = lax.dynamic_slice_in_dim(voltages, start, CH_DEV, 2).astype(jnp.float32)
        summed = lax.optimization_barrier(jnp.sum(block, axis=0))
        power = summed[0] * summed[0] + summed[1] * summed[1]
        level = lax.optimization_barrier(jnp.mean(power, axis=1, keepdims=True))
        intensity = jnp.transpose(power / (level + epsilon) - 1.0, (1, 2, 0))
        own = lax.dynamic_slice_in_dim(fine_delays, start, CH_DEV, 1)
        local = jnp.zeros((BEAMS, span, NG), jnp.float32)
        for delay in range(FINE_MAX + 1):
            chosen = (own == delay).astype(jnp.float32)
            local = local + jnp.einsum('tbc,gc->btg', intensity[delay:delay + span], chosen, precision=lax.Precision.HIGHEST)
        return local
    partial_value = lax.map(one_band, jnp.arange(SUBBANDS, dtype=jnp.int32))
    codes = coarse_delays.reshape(NG, per_group, SUBBANDS)
    series = jnp.zeros((BEAMS, length, NG, per_group), jnp.float32)
    for delay in range(COARSE_MAX + 1):
        chosen = (codes == delay).astype(jnp.float32)
        series = series + jnp.einsum('sbtg,gjs->btgj', partial_value[:, :, delay:delay + length], chosen, precision=lax.Precision.HIGHEST)
    series = series.reshape(BEAMS, length, NDM)
    return boxcar_search(series, CHANNELS)
```

```python
import functools
import math

import jax
import jax.numpy as jnp
from jax import lax
from jax.experimental import pallas as pl
from jax.experimental.pallas import tpu as pltpu
from jax.sharding import PartitionSpec as P

FINE_MAX = 8
COARSE_MAX = 16
NWID = 4
MESH = pl.DeviceIdType.MESH

epsilon = 1e-06
PART = 8
BLOCK = 16
LANES = 128


def gather_lanes(x, index):
    numbers = lax.GatherDimensionNumbers(
        offset_dims=(),
        collapsed_slice_dims=(1,),
        start_index_map=(1,),
        operand_batching_dims=(0,),
        start_indices_batching_dims=(0,),
    )
    return lax.gather(
        x, index[..., None], numbers, (1, 1), mode=lax.GatherScatterMode.PROMISE_IN_BOUNDS
    )


def kernel(
    bands, total_channels,
    v_hbm, fine_hbm, coarse_hbm, out_ref,
    v, s1, r1, r2, xt, xhl, mask, fd, cd, cdt, idx, o, m, r3,
    load_sem, side_sem, d_send, d_recv, z_send, z_recv, a_send, a_recv,
):
    parts = v.shape[1]
    samples = v.shape[4]
    lanes = v.shape[5]
    rows = PART * samples
    groups = fd.shape[0]
    width = fd.shape[1]
    span = samples - FINE_MAX
    per_group = cd.shape[0] // groups
    rowsets = cd.shape[0] // LANES
    feed = lax.axis_index("feed")
    me = lax.axis_index("chan")
    core, low = lax.rem(feed, 2), lax.div(feed, 2)

    def quarter(r):
        return lax.rem(low + r // 2, 2) * 2 + lax.rem(core + r % 2, 2)

    core_peer, chip_peer = quarter(1), quarter(2)

    def load(i, r):
        return pltpu.make_async_copy(
            v_hbm.at[0, :, pl.ds(i * PART, PART), :, pl.ds(pl.multiple_of(quarter(r) * lanes, lanes), lanes)],
            v.at[r, i],
            load_sem.at[i * 4 + r],
        )

    def to_core(i, p):
        return pltpu.make_async_remote_copy(
            src_ref=s1.at[i, p], dst_ref=r1.at[i, p],
            send_sem=d_send.at[i * 2 + p], recv_sem=d_recv.at[i * 2 + p],
            device_id=(core_peer, me), device_id_type=MESH,
        )

    def to_chip(i):
        return pltpu.make_async_remote_copy(
            src_ref=r1.at[i, 1], dst_ref=r2.at[i],
            send_sem=z_send.at[i], recv_sem=z_recv.at[i],
            device_id=(chip_peer, me), device_id_type=MESH,
        )

    def to_band(k, slot):
        return pltpu.make_async_remote_copy(
            src_ref=m.at[pl.ds(pl.multiple_of(k * 16, 16), 16)],
            dst_ref=r3.at[pl.ds(pl.multiple_of(slot * 16, 16), 16)],
            send_sem=a_send.at[k], recv_sem=a_recv.at[slot],
            device_id=(feed, k), device_id_type=MESH,
        )

    @pl.loop(0, parts)
    def _(i):
        for r in (3, 1, 2, 0):
            load(i, r).start()

    own_fine = pltpu.make_async_copy(
        fine_hbm.at[:, pl.ds(pl.multiple_of(me * width, width), width)], fd, side_sem.at[0]
    )
    own_fine.start()
    all_coarse = pltpu.make_async_copy(coarse_hbm, cd, side_sem.at[1])
    all_coarse.start()

    barrier = pltpu.get_barrier_semaphore()
    pl.semaphore_signal(barrier, inc=1, device_id=(core_peer, me), device_id_type=MESH)
    pl.semaphore_signal(barrier, inc=1, device_id=(chip_peer, me), device_id_type=MESH)

    @pl.loop(1, bands)
    def _(away):
        pl.semaphore_signal(
            barrier, inc=1, device_id=(feed, lax.rem(me + away, bands)), device_id_type=MESH
        )

    def widen(i):
        for r, p in ((3, 1), (1, 0)):
            load(i, r).wait()
            s1[i, p] = v[r, i].astype(jnp.float32).reshape(2, rows, lanes)

    def send_core(i):
        to_core(i, 1).start()
        to_core(i, 0).start()

    def pass_on(i):
        load(i, 2).wait()
        to_core(i, 1).wait_recv()
        r1[i, 1] = r1[i, 1] + v[2, i].astype(jnp.float32).reshape(2, rows, lanes)
        to_chip(i).start()

    widen(0)
    pl.semaphore_wait(barrier, bands + 1)
    send_core(0)

    @pl.loop(1, parts)
    def _(i):
        widen(i)
        send_core(i)
        pass_on(i - 1)

    pass_on(parts - 1)

    own_fine.wait()
    for delay in range(FINE_MAX + 1):
        chosen = jnp.where(fd[...] == delay, 1.0, 0.0).astype(jnp.bfloat16)
        mask[delay * groups : (delay + 1) * groups, :width] = chosen
        mask[delay * groups : (delay + 1) * groups, width:] = chosen

    all_coarse.wait()
    for q in range(rowsets):
        cdt[pl.ds(q, bands, stride=rowsets), :] = cd[q * LANES : (q + 1) * LANES, :].T
    lane = lax.broadcasted_iota(jnp.int32, (rowsets, LANES), 1)
    base = lane - lax.rem(lane, span) + lax.rem(lane, 16)
    first = lane - lax.rem(lane, 16)

    @pl.loop(0, bands)
    def _(s):
        codes = cdt[pl.ds(pl.multiple_of(s * rowsets, rowsets), rowsets), :]
        for j in range(16):
            idx[s * 16 + j] = base + gather_lanes(codes, first + j)

    def normalise(i, place):
        to_core(i, 0).wait_recv()
        load(i, 0).wait()
        to_chip(i).wait_recv()
        power = None
        for c in range(2):
            total = r1[i, 0, c] + v[0, i, c].astype(jnp.float32).reshape(rows, lanes) + r2[i, c]
            power = total * total if power is None else power + total * total
        power = power.reshape(PART, samples, lanes)
        level = jnp.sum(power, axis=1, keepdims=True) * (1.0 / samples)
        value = power * (1.0 / (level + epsilon)) - 1.0
        xt[place * rows : (place + 1) * rows, :] = value.reshape(rows, lanes)

    @pl.loop(0, parts * PART // BLOCK)
    def _(g):
        for place in range(BLOCK // PART):
            normalise(g * (BLOCK // PART) + place, place)
        for t in range(samples):
            value = xt[pl.ds(t, BLOCK, stride=samples), :]
            high = value.astype(jnp.bfloat16)
            low_part = (value - high.astype(jnp.float32)).astype(jnp.bfloat16)
            xhl[t, pl.ds(pl.multiple_of(g * BLOCK, BLOCK), BLOCK), :] = high
            xhl[t, pl.ds(pl.multiple_of(width + g * BLOCK, BLOCK), BLOCK), :] = low_part

    @pl.loop(0, parts)
    def _(i):
        to_core(i, 0).wait_send()
        to_core(i, 1).wait_send()

    terms = (FINE_MAX + 1) * groups

    @pl.loop(0, samples // 4)
    def _(i):
        for p in range(2):
            both = jnp.concatenate([xhl[i * 4 + p * 2], xhl[i * 4 + p * 2 + 1]], axis=1)
            product = jnp.dot(mask[...], both, preferred_element_type=jnp.float32)
            s1[i, p, 0, :terms, :] = product[:, :lanes]
            s1[i, p, 1, :terms, :] = product[:, lanes:]

    for t in range(span):
        total = None
        for delay in range(FINE_MAX + 1):
            at = t + delay
            term = s1[at // 4, at // 2 % 2, at % 2, delay * groups : (delay + 1) * groups, :]
            total = term if total is None else total + term
        o[pl.ds(t, groups, stride=span), :] = total

    for q in range(rowsets):
        m[pl.ds(q, lanes, stride=rowsets), :] = o[q * LANES : (q + 1) * LANES, :].T

    @pl.loop(1, bands)
    def _(away):
        to_band(lax.rem(me + away, bands), me).start()

    mine = pl.ds(pl.multiple_of(me * 16, 16), 16)
    r3[mine, :] = m[mine, :]

    def collect(s, totals):
        totals = list(totals)
        pair = [
            r3[pl.ds(pl.multiple_of(s * 16 + b * rowsets, rowsets), rowsets), :] for b in range(2)
        ]
        for j in range(16):
            index = idx[s * 16 + j]
            for b in range(2):
                totals[b * 16 + j] = totals[b * 16 + j] + gather_lanes(pair[b], index)
        return tuple(totals)

    def step(away, totals):
        s = lax.rem(me + bands - away, bands)
        to_band(s, s).wait_recv()
        return collect(s, totals)

    totals = collect(me, (jnp.zeros((rowsets, LANES), jnp.float32),) * 32)
    totals = lax.fori_loop(1, bands, step, totals)

    sample = lax.rem(lane, 16)

    def ahead(x, n):
        return pltpu.roll(x, LANES - n, 1)

    for b in range(2):
        best = [jnp.zeros((rowsets, LANES), jnp.float32)] * NWID
        for j in range(16):
            box = totals[b * 16 + j]
            for k in range(NWID):
                high = jnp.where(sample <= 16 - 2**k, box, -jnp.inf)
                for n in (8, 4, 2, 1):
                    high = jnp.maximum(high, ahead(high, n))
                if j:
                    high = pltpu.roll(high, j, 1)
                best[k] = jnp.where(sample == j, high, best[k])
                if k + 1 < NWID:
                    box = box + ahead(box, 2**k)
        for k in range(NWID):
            result = best[k] * (1.0 / math.sqrt(2**k * total_channels))
            for q in range(rowsets):
                out_ref[k, b : b + 1, q * LANES : (q + 1) * LANES] = result[q : q + 1, :]

    @pl.loop(1, bands)
    def _(away):
        k = lax.rem(me + away, bands)
        to_band(k, k).wait_send()

    @pl.loop(0, parts)
    def _(i):
        to_chip(i).wait_send()


def local(voltages, fine_delays, coarse_delays):
    _, _, channels, samples, beams = voltages.shape
    groups, total_channels = fine_delays.shape
    trials, bands = coarse_delays.shape
    lanes = beams // lax.axis_size("feed")
    parts = channels // PART
    rows = PART * samples
    f32, bf16, i32 = jnp.float32, jnp.bfloat16, jnp.int32
    dma = pltpu.SemaphoreType.DMA
    vmem = pltpu.VMEM
    return pl.pallas_call(
        functools.partial(kernel, bands, total_channels),
        out_shape=jax.ShapeDtypeStruct((NWID, beams // (lax.axis_size("feed") * bands), trials), f32),
        in_specs=[pl.BlockSpec(memory_space=pl.ANY)] * 3,
        out_specs=pl.BlockSpec(memory_space=pltpu.VMEM),
        scratch_shapes=[
            vmem((4, parts, 2, PART, samples, lanes), bf16),
            vmem((parts, 2, 2, rows, lanes), f32),
            vmem((parts, 2, 2, rows, lanes), f32),
            vmem((parts, 2, rows, lanes), f32),
            vmem((BLOCK * samples, lanes), f32),
            vmem((samples, 2 * channels, lanes), bf16),
            vmem(((FINE_MAX + 1) * groups, 2 * channels), bf16),
            vmem((groups, channels), i32),
            vmem((trials, bands), i32),
            vmem((bands * trials // LANES, LANES), i32),
            vmem((bands * 16, trials // LANES, LANES), i32),
            vmem((groups * (samples - FINE_MAX), lanes), f32),
            vmem((lanes * trials // LANES, LANES), f32),
            vmem((bands * 16, LANES), f32),
            dma((parts * 4,)),
            dma((2,)),
            dma((parts * 2,)),
            dma((parts * 2,)),
            dma((parts,)),
            dma((parts,)),
            dma((bands,)),
            dma((bands,)),
        ],
        compiler_params=pltpu.CompilerParams(
            collective_id=0, has_side_effects=True, vmem_limit_bytes=60 * 1024 * 1024
        ),
        cost_estimate=pl.CostEstimate(flops=10**9, bytes_accessed=11 * 10**6, transcendentals=0),
    )(voltages, fine_delays, coarse_delays)


def solution(mesh):
    in_specs = (P("feed", None, "chan", None, None), P(), P())
    out_specs = P(None, ("feed", "chan"), None)
    return jax.shard_map(local, mesh=mesh, in_specs=in_specs, out_specs=out_specs, check_vma=False)
```

```python
import functools
import math

import jax
import jax.numpy as jnp
from jax import lax
from jax.experimental import pallas as pl
from jax.experimental.pallas import tpu as pltpu
from jax.sharding import PartitionSpec as P

FINE_MAX = 8
COARSE_MAX = 16
NWID = 4
MESH = pl.DeviceIdType.MESH

epsilon = 1e-06
PART = 8
BLOCK = 16
LANES = 128
AHEAD = 4


def gather_lanes(x, index):
    numbers = lax.GatherDimensionNumbers(
        offset_dims=(),
        collapsed_slice_dims=(1,),
        start_index_map=(1,),
        operand_batching_dims=(0,),
        start_indices_batching_dims=(0,),
    )
    return lax.gather(
        x, index[..., None], numbers, (1, 1), mode=lax.GatherScatterMode.PROMISE_IN_BOUNDS
    )


def kernel(
    bands, total_channels,
    v_hbm, fine_hbm, coarse_hbm, out_ref,
    v, s1, r1, r2, xt, xhl, mask, fd, cd, cdt, idx, o, m, r3,
    load_sem, side_sem, d_send, d_recv, z_send, z_recv, a_send, a_recv, met_sem,
):
    parts = v.shape[1]
    samples = v.shape[4]
    lanes = v.shape[5]
    rows = PART * samples
    groups = fd.shape[0]
    width = fd.shape[1]
    span = samples - FINE_MAX
    rowsets = cd.shape[1] // LANES
    feed = lax.axis_index("feed")
    me = lax.axis_index("chan")
    core, low = lax.rem(feed, 2), lax.div(feed, 2)

    def quarter(r):
        return lax.rem(low + r // 2, 2) * 2 + lax.rem(core + r % 2, 2)

    core_peer, chip_peer = quarter(1), quarter(2)

    def load(i, r):
        return pltpu.make_async_copy(
            v_hbm.at[0, :, pl.ds(i * PART, PART), :, pl.ds(pl.multiple_of(quarter(r) * lanes, lanes), lanes)],
            v.at[r, i],
            load_sem.at[i * 4 + r],
        )

    def to_core(i, p):
        return pltpu.make_async_remote_copy(
            src_ref=s1.at[i, p], dst_ref=r1.at[i, p],
            send_sem=d_send.at[i * 2 + p], recv_sem=d_recv.at[i * 2 + p],
            device_id=(core_peer, me), device_id_type=MESH,
        )

    def to_chip(i):
        return pltpu.make_async_remote_copy(
            src_ref=r1.at[i, 1], dst_ref=r2.at[i],
            send_sem=z_send.at[i], recv_sem=z_recv.at[i],
            device_id=(chip_peer, me), device_id_type=MESH,
        )

    def to_band(k, slot):
        return pltpu.make_async_remote_copy(
            src_ref=m.at[pl.ds(pl.multiple_of(k * 16, 16), 16)],
            dst_ref=r3.at[pl.ds(pl.multiple_of(slot * 16, 16), 16)],
            send_sem=a_send.at[k], recv_sem=a_recv.at[slot],
            device_id=(feed, k), device_id_type=MESH,
        )

    def fetch(i):
        for r in (3, 1, 2, 0):
            load(i, r).start()

    fetch(0)

    barrier = pltpu.get_barrier_semaphore()
    pl.semaphore_signal(barrier, inc=1, device_id=(core_peer, me), device_id_type=MESH)
    pl.semaphore_signal(barrier, inc=1, device_id=(chip_peer, me), device_id_type=MESH)

    ring = min(bands, 4)
    digit = lax.rem(me, ring)
    friends = [[me - digit + lax.rem(digit + 1, ring)]]
    if ring > 2:
        friends[0].append(me - digit + lax.rem(digit + ring - 1, ring))
    bit = ring
    while bit < bands:
        friends.append([me + (1 - 2 * lax.rem(lax.div(me, bit), 2)) * bit])
        bit *= 2
    for turn in friends:
        for k in turn:
            pl.semaphore_signal(barrier, inc=1, device_id=(feed, k), device_id_type=MESH)
    for i in range(1, AHEAD):
        fetch(i)
    own_fine = pltpu.make_async_copy(
        fine_hbm.at[:, pl.ds(pl.multiple_of(me * width, width), width)], fd, side_sem.at[0]
    )
    own_fine.start()
    all_coarse = pltpu.make_async_copy(coarse_hbm, cd, side_sem.at[1])
    all_coarse.start()

    def widen(i, r, p):
        load(i, r).wait()
        s1[i, p] = v[r, i].astype(jnp.float32).reshape(2, rows, lanes)

    def pass_on(i):
        load(i, 2).wait()
        to_core(i, 1).wait_recv()
        r1[i, 1] = r1[i, 1] + v[2, i].astype(jnp.float32).reshape(2, rows, lanes)
        to_chip(i).start()

    widen(0, 3, 1)
    widen(0, 1, 0)
    pl.semaphore_wait(barrier, 2 + sum(len(turn) for turn in friends))
    to_core(0, 1).start()
    to_core(0, 0).start()

    @pl.loop(1, parts)
    def _(i):
        @pl.when(i + AHEAD - 1 < parts)
        def _():
            fetch(i + AHEAD - 1)

        for r, p in ((3, 1), (1, 0)):
            widen(i, r, p)
            to_core(i, p).start()
        pass_on(i - 1)

    pass_on(parts - 1)

    for turn, ks in enumerate(friends):
        if turn or ring > 2:
            for k in ks:
                pl.semaphore_signal(
                    met_sem.at[turn], inc=1, device_id=(feed, k), device_id_type=MESH
                )
            pl.semaphore_wait(met_sem.at[turn], len(ks))

    own_fine.wait()
    for delay in range(FINE_MAX + 1):
        chosen = jnp.where(fd[...] == delay, 1.0, 0.0).astype(jnp.bfloat16)
        mask[delay * groups : (delay + 1) * groups, :width] = chosen
        mask[delay * groups : (delay + 1) * groups, width:] = chosen

    all_coarse.wait()
    for q in range(rowsets):
        cdt[pl.ds(q, bands, stride=rowsets), :] = cd[:, q * LANES : (q + 1) * LANES]
    lane = lax.broadcasted_iota(jnp.int32, (rowsets, LANES), 1)
    base = lane - lax.rem(lane, span) + lax.rem(lane, 16)
    first = lane - lax.rem(lane, 16)

    @pl.loop(0, bands)
    def _(s):
        codes = cdt[pl.ds(pl.multiple_of(s * rowsets, rowsets), rowsets), :]
        for j in range(16):
            idx[s * 16 + j] = base + gather_lanes(codes, first + j)

    def normalise(i, place):
        to_core(i, 0).wait_recv()
        load(i, 0).wait()
        to_chip(i).wait_recv()
        power = None
        for c in range(2):
            total = r1[i, 0, c] + v[0, i, c].astype(jnp.float32).reshape(rows, lanes) + r2[i, c]
            power = total * total if power is None else power + total * total
        power = power.reshape(PART, samples, lanes)
        level = jnp.sum(power, axis=1, keepdims=True) * (1.0 / samples)
        value = power * (1.0 / (level + epsilon)) - 1.0
        xt[place * rows : (place + 1) * rows, :] = value.reshape(rows, lanes)

    @pl.loop(0, parts * PART // BLOCK)
    def _(g):
        for place in range(BLOCK // PART):
            normalise(g * (BLOCK // PART) + place, place)
        for t in range(samples):
            value = xt[pl.ds(t, BLOCK, stride=samples), :]
            high = value.astype(jnp.bfloat16)
            low_part = (value - high.astype(jnp.float32)).astype(jnp.bfloat16)
            xhl[t, pl.ds(pl.multiple_of(g * BLOCK, BLOCK), BLOCK), :] = high
            xhl[t, pl.ds(pl.multiple_of(width + g * BLOCK, BLOCK), BLOCK), :] = low_part

    @pl.loop(0, parts)
    def _(i):
        to_core(i, 0).wait_send()
        to_core(i, 1).wait_send()

    terms = (FINE_MAX + 1) * groups

    @pl.loop(0, samples // 4)
    def _(i):
        for p in range(2):
            both = jnp.concatenate([xhl[i * 4 + p * 2], xhl[i * 4 + p * 2 + 1]], axis=1)
            product = jnp.dot(mask[...], both, preferred_element_type=jnp.float32)
            s1[i, p, 0, :terms, :] = product[:, :lanes]
            s1[i, p, 1, :terms, :] = product[:, lanes:]

    for t in range(span):
        total = None
        for delay in range(FINE_MAX + 1):
            at = t + delay
            term = s1[at // 4, at // 2 % 2, at % 2, delay * groups : (delay + 1) * groups, :]
            total = term if total is None else total + term
        o[pl.ds(t, groups, stride=span), :] = total

    for q in range(rowsets):
        m[pl.ds(q, lanes, stride=rowsets), :] = o[q * LANES : (q + 1) * LANES, :].T

    @pl.loop(1, bands)
    def _(away):
        to_band(lax.rem(me + away, bands), me).start()

    mine = pl.ds(pl.multiple_of(me * 16, 16), 16)
    r3[mine, :] = m[mine, :]

    def collect(s, totals):
        totals = list(totals)
        pair = [
            r3[pl.ds(pl.multiple_of(s * 16 + b * rowsets, rowsets), rowsets), :] for b in range(2)
        ]
        for j in range(16):
            index = idx[s * 16 + j]
            for b in range(2):
                totals[b * 16 + j] = totals[b * 16 + j] + gather_lanes(pair[b], index)
        return tuple(totals)

    def step(away, totals):
        s = lax.rem(me + bands - away, bands)
        to_band(s, s).wait_recv()
        return collect(s, totals)

    totals = collect(me, (jnp.zeros((rowsets, LANES), jnp.float32),) * 32)
    totals = lax.fori_loop(1, bands, step, totals)

    box = jnp.concatenate([totals[b * 16 + j] for j in range(16) for b in range(2)], axis=0)

    def sample_of(x):
        return lax.rem(lax.broadcasted_iota(jnp.int32, x.shape, 1), 16)

    def ahead(x, n):
        return pltpu.roll(x, LANES - n, 1)

    for k in range(NWID):
        best = jnp.where(sample_of(box) <= 16 - 2**k, box, -jnp.inf)
        for n in (8, 4, 2, 1):
            half = best.shape[0] // 2
            a, b = best[:half], best[half:]
            upper = lax.rem(lax.div(sample_of(a), n), 2) == 1
            best = jnp.maximum(
                jnp.where(upper, pltpu.roll(b, n, 1), a), jnp.where(upper, b, ahead(a, n))
            )
        result = best * (1.0 / math.sqrt(2**k * total_channels))
        for b in range(2):
            for q in range(rowsets):
                row = b * rowsets + q
                out_ref[k, b : b + 1, q * LANES : (q + 1) * LANES] = result[row : row + 1, :]
        if k + 1 < NWID:
            box = box + ahead(box, 2**k)

    @pl.loop(1, bands)
    def _(away):
        k = lax.rem(me + away, bands)
        to_band(k, k).wait_send()

    @pl.loop(0, parts)
    def _(i):
        to_chip(i).wait_send()


def local(voltages, fine_delays, coarse_delays):
    _, _, channels, samples, beams = voltages.shape
    groups, total_channels = fine_delays.shape
    trials, bands = coarse_delays.shape
    lanes = beams // lax.axis_size("feed")
    parts = channels // PART
    rows = PART * samples
    f32, bf16, i32 = jnp.float32, jnp.bfloat16, jnp.int32
    dma = pltpu.SemaphoreType.DMA
    vmem = pltpu.VMEM
    return pl.pallas_call(
        functools.partial(kernel, bands, total_channels),
        out_shape=jax.ShapeDtypeStruct((NWID, beams // (lax.axis_size("feed") * bands), trials), f32),
        in_specs=[pl.BlockSpec(memory_space=pl.ANY)] * 3,
        out_specs=pl.BlockSpec(memory_space=pltpu.VMEM),
        scratch_shapes=[
            vmem((4, parts, 2, PART, samples, lanes), bf16),
            vmem((parts, 2, 2, rows, lanes), f32),
            vmem((parts, 2, 2, rows, lanes), f32),
            vmem((parts, 2, rows, lanes), f32),
            vmem((BLOCK * samples, lanes), f32),
            vmem((samples, 2 * channels, lanes), bf16),
            vmem(((FINE_MAX + 1) * groups, 2 * channels), bf16),
            vmem((groups, channels), i32),
            vmem((bands, trials), i32),
            vmem((bands * trials // LANES, LANES), i32),
            vmem((bands * 16, trials // LANES, LANES), i32),
            vmem((groups * (samples - FINE_MAX), lanes), f32),
            vmem((lanes * trials // LANES, LANES), f32),
            vmem((bands * 16, LANES), f32),
            dma((parts * 4,)),
            dma((2,)),
            dma((parts * 2,)),
            dma((parts * 2,)),
            dma((parts,)),
            dma((parts,)),
            dma((bands,)),
            dma((bands,)),
            pltpu.SemaphoreType.REGULAR((8,)),
        ],
        compiler_params=pltpu.CompilerParams(
            collective_id=0, has_side_effects=True, vmem_limit_bytes=60 * 1024 * 1024
        ),
        cost_estimate=pl.CostEstimate(flops=10**9, bytes_accessed=11 * 10**6, transcendentals=0),
    )(voltages, fine_delays, coarse_delays.T)


def solution(mesh):
    in_specs = (P("feed", None, "chan", None, None), P(), P())
    out_specs = P(None, ("feed", "chan"), None)
    return jax.shard_map(local, mesh=mesh, in_specs=in_specs, out_specs=out_specs, check_vma=False)
```

```python
import functools
import math

import jax
import jax.numpy as jnp
from jax import lax
from jax.experimental import pallas as pl
from jax.experimental.pallas import tpu as pltpu
from jax.sharding import PartitionSpec as P

FINE_MAX = 8
COARSE_MAX = 16
NWID = 4
MESH = pl.DeviceIdType.MESH

epsilon = 1e-06
PART = 8
BLOCK = 16
LANES = 128
AHEAD = 4


def gather_lanes(x, index):
    numbers = lax.GatherDimensionNumbers(
        offset_dims=(),
        collapsed_slice_dims=(1,),
        start_index_map=(1,),
        operand_batching_dims=(0,),
        start_indices_batching_dims=(0,),
    )
    return lax.gather(
        x, index[..., None], numbers, (1, 1), mode=lax.GatherScatterMode.PROMISE_IN_BOUNDS
    )


def kernel(
    bands, total_channels,
    v_hbm, fine_hbm, coarse_hbm, out_ref,
    v, s1, r1, r2, xt, xhl, mask, fd, cd, cdt, idx, o, m, r3,
    load_sem, side_sem, d_send, d_recv, z_send, z_recv, a_send, a_recv, met_sem,
):
    parts = v.shape[1]
    samples = v.shape[4]
    lanes = v.shape[5]
    rows = PART * samples
    groups = fd.shape[0]
    width = fd.shape[1]
    span = samples - FINE_MAX
    rowsets = cd.shape[1] // LANES
    feed = lax.axis_index("feed")
    me = lax.axis_index("chan")
    core, low = lax.rem(feed, 2), lax.div(feed, 2)

    def quarter(r):
        return lax.rem(low + r // 2, 2) * 2 + lax.rem(core + r % 2, 2)

    core_peer, chip_peer = quarter(1), quarter(2)

    def load(i, r):
        return pltpu.make_async_copy(
            v_hbm.at[0, :, pl.ds(i * PART, PART), :, pl.ds(pl.multiple_of(quarter(r) * lanes, lanes), lanes)],
            v.at[r, i],
            load_sem.at[i * 4 + r],
        )

    def to_core(i, p):
        return pltpu.make_async_remote_copy(
            src_ref=s1.at[i, p], dst_ref=r1.at[i, p],
            send_sem=d_send.at[i * 2 + p], recv_sem=d_recv.at[i * 2 + p],
            device_id=(core_peer, me), device_id_type=MESH,
        )

    def to_chip(i):
        return pltpu.make_async_remote_copy(
            src_ref=r1.at[i, 1], dst_ref=r2.at[i],
            send_sem=z_send.at[i], recv_sem=z_recv.at[i],
            device_id=(chip_peer, me), device_id_type=MESH,
        )

    def to_band(k, slot):
        return pltpu.make_async_remote_copy(
            src_ref=m.at[pl.ds(pl.multiple_of(k * 16, 16), 16)],
            dst_ref=r3.at[pl.ds(pl.multiple_of(slot * 16, 16), 16)],
            send_sem=a_send.at[k], recv_sem=a_recv.at[slot],
            device_id=(feed, k), device_id_type=MESH,
        )

    def fetch(i):
        for r in (3, 1, 2, 0):
            load(i, r).start()

    fetch(0)

    barrier = pltpu.get_barrier_semaphore()
    pl.semaphore_signal(barrier, inc=1, device_id=(core_peer, me), device_id_type=MESH)
    pl.semaphore_signal(barrier, inc=1, device_id=(chip_peer, me), device_id_type=MESH)

    ring = min(bands, 4)
    digit = lax.rem(me, ring)
    friends = [[me - digit + lax.rem(digit + 1, ring)]]
    if ring > 2:
        friends[0].append(me - digit + lax.rem(digit + ring - 1, ring))
    bit = ring
    while bit < bands:
        friends.append([me + (1 - 2 * lax.rem(lax.div(me, bit), 2)) * bit])
        bit *= 2
    for turn in friends:
        for k in turn:
            pl.semaphore_signal(barrier, inc=1, device_id=(feed, k), device_id_type=MESH)
    for i in range(1, AHEAD):
        fetch(i)
    own_fine = pltpu.make_async_copy(
        fine_hbm.at[:, pl.ds(pl.multiple_of(me * width, width), width)], fd, side_sem.at[0]
    )
    own_fine.start()
    all_coarse = pltpu.make_async_copy(coarse_hbm, cd, side_sem.at[1])
    all_coarse.start()

    def widen(i, r, p):
        load(i, r).wait()
        s1[i, p] = v[r, i].astype(jnp.float32).reshape(2, rows, lanes)

    def pass_on(i):
        load(i, 2).wait()
        to_core(i, 1).wait_recv()
        r1[i, 1] = r1[i, 1] + v[2, i].astype(jnp.float32).reshape(2, rows, lanes)
        to_chip(i).start()

    widen(0, 3, 1)
    widen(0, 1, 0)
    pl.semaphore_wait(barrier, 2 + sum(len(turn) for turn in friends))
    to_core(0, 1).start()
    to_core(0, 0).start()

    @pl.loop(1, parts)
    def _(i):
        @pl.when(i + AHEAD - 1 < parts)
        def _():
            fetch(i + AHEAD - 1)

        for r, p in ((3, 1), (1, 0)):
            widen(i, r, p)
            to_core(i, p).start()
        pass_on(i - 1)

    pass_on(parts - 1)

    for turn, ks in enumerate(friends):
        if turn or ring > 2:
            for k in ks:
                pl.semaphore_signal(
                    met_sem.at[turn], inc=1, device_id=(feed, k), device_id_type=MESH
                )
            pl.semaphore_wait(met_sem.at[turn], len(ks))

    own_fine.wait()
    for delay in range(FINE_MAX + 1):
        chosen = jnp.where(fd[...] == delay, 1.0, 0.0).astype(jnp.bfloat16)
        mask[delay * groups : (delay + 1) * groups, :width] = chosen
        mask[delay * groups : (delay + 1) * groups, width:] = chosen

    all_coarse.wait()
    for q in range(rowsets):
        cdt[pl.ds(q, bands, stride=rowsets), :] = cd[:, q * LANES : (q + 1) * LANES]
    lane = lax.broadcasted_iota(jnp.int32, (rowsets, LANES), 1)
    base = lane - lax.rem(lane, span) + lax.rem(lane, 16)
    first = lane - lax.rem(lane, 16)

    @pl.loop(0, bands)
    def _(s):
        codes = cdt[pl.ds(pl.multiple_of(s * rowsets, rowsets), rowsets), :]
        for j in range(16):
            idx[s * 16 + j] = base + gather_lanes(codes, first + j)

    def normalise(i, place):
        to_core(i, 0).wait_recv()
        load(i, 0).wait()
        to_chip(i).wait_recv()
        power = None
        for c in range(2):
            total = r1[i, 0, c] + v[0, i, c].astype(jnp.float32).reshape(rows, lanes) + r2[i, c]
            power = total * total if power is None else power + total * total
        power = power.reshape(PART, samples, lanes)
        level = jnp.sum(power, axis=1, keepdims=True) * (1.0 / samples)
        value = power * (1.0 / (level + epsilon)) - 1.0
        xt[place * rows : (place + 1) * rows, :] = value.reshape(rows, lanes)

    @pl.loop(0, parts * PART // BLOCK)
    def _(g):
        for place in range(BLOCK // PART):
            normalise(g * (BLOCK // PART) + place, place)
        for t in range(samples):
            value = xt[pl.ds(t, BLOCK, stride=samples), :]
            high = value.astype(jnp.bfloat16)
            low_part = (value - high.astype(jnp.float32)).astype(jnp.bfloat16)
            xhl[t, pl.ds(pl.multiple_of(g * BLOCK, BLOCK), BLOCK), :] = high
            xhl[t, pl.ds(pl.multiple_of(width + g * BLOCK, BLOCK), BLOCK), :] = low_part

    @pl.loop(0, parts)
    def _(i):
        to_core(i, 0).wait_send()
        to_core(i, 1).wait_send()

    terms = (FINE_MAX + 1) * groups

    for i in range(samples // 4):
        for p in range(2):
            both = jnp.concatenate([xhl[i * 4 + p * 2], xhl[i * 4 + p * 2 + 1]], axis=1)
            product = jnp.dot(mask[...], both, preferred_element_type=jnp.float32)
            s1[i, p, 0, :terms, :] = product[:, :lanes]
            s1[i, p, 1, :terms, :] = product[:, lanes:]

    for t in range(span):
        total = None
        for delay in range(FINE_MAX + 1):
            at = t + delay
            term = s1[at // 4, at // 2 % 2, at % 2, delay * groups : (delay + 1) * groups, :]
            total = term if total is None else total + term
        o[pl.ds(t, groups, stride=span), :] = total

    for q in range(rowsets):
        m[pl.ds(q, lanes, stride=rowsets), :] = o[q * LANES : (q + 1) * LANES, :].T

    @pl.loop(1, bands)
    def _(away):
        to_band(lax.rem(me + away, bands), me).start()

    mine = pl.ds(pl.multiple_of(me * 16, 16), 16)
    r3[mine, :] = m[mine, :]

    def collect(s, totals):
        totals = list(totals)
        pair = [
            r3[pl.ds(pl.multiple_of(s * 16 + b * rowsets, rowsets), rowsets), :] for b in range(2)
        ]
        for j in range(16):
            index = idx[s * 16 + j]
            for b in range(2):
                totals[b * 16 + j] = totals[b * 16 + j] + gather_lanes(pair[b], index)
        return tuple(totals)

    together = max(n for n in range(1, 8) if (bands - 1) % n == 0)

    def step(turn, totals):
        sources = [lax.rem(me + bands - 1 - turn * together - n, bands) for n in range(together)]
        for s in sources:
            to_band(s, s).wait_recv()
        for s in sources:
            totals = collect(s, totals)
        return totals

    totals = collect(me, (jnp.zeros((rowsets, LANES), jnp.float32),) * 32)
    totals = lax.fori_loop(0, (bands - 1) // together, step, totals)

    box = jnp.concatenate([totals[b * 16 + j] for j in range(16) for b in range(2)], axis=0)

    def sample_of(x):
        return lax.rem(lax.broadcasted_iota(jnp.int32, x.shape, 1), 16)

    def ahead(x, n):
        return pltpu.roll(x, LANES - n, 1)

    for k in range(NWID):
        best = jnp.where(sample_of(box) <= 16 - 2**k, box, -jnp.inf)
        for n in (8, 4, 2, 1):
            half = best.shape[0] // 2
            a, b = best[:half], best[half:]
            upper = lax.rem(lax.div(sample_of(a), n), 2) == 1
            best = jnp.maximum(
                jnp.where(upper, pltpu.roll(b, n, 1), a), jnp.where(upper, b, ahead(a, n))
            )
        result = best * (1.0 / math.sqrt(2**k * total_channels))
        for b in range(2):
            for q in range(rowsets):
                row = b * rowsets + q
                out_ref[k, b : b + 1, q * LANES : (q + 1) * LANES] = result[row : row + 1, :]
        if k + 1 < NWID:
            box = box + ahead(box, 2**k)

    @pl.loop(1, bands)
    def _(away):
        k = lax.rem(me + away, bands)
        to_band(k, k).wait_send()

    @pl.loop(0, parts)
    def _(i):
        to_chip(i).wait_send()


def local(voltages, fine_delays, coarse_delays):
    _, _, channels, samples, beams = voltages.shape
    groups, total_channels = fine_delays.shape
    trials, bands = coarse_delays.shape
    lanes = beams // lax.axis_size("feed")
    parts = channels // PART
    rows = PART * samples
    f32, bf16, i32 = jnp.float32, jnp.bfloat16, jnp.int32
    dma = pltpu.SemaphoreType.DMA
    vmem = pltpu.VMEM
    return pl.pallas_call(
        functools.partial(kernel, bands, total_channels),
        out_shape=jax.ShapeDtypeStruct((NWID, beams // (lax.axis_size("feed") * bands), trials), f32),
        in_specs=[pl.BlockSpec(memory_space=pl.ANY)] * 3,
        out_specs=pl.BlockSpec(memory_space=pltpu.VMEM),
        scratch_shapes=[
            vmem((4, parts, 2, PART, samples, lanes), bf16),
            vmem((parts, 2, 2, rows, lanes), f32),
            vmem((parts, 2, 2, rows, lanes), f32),
            vmem((parts, 2, rows, lanes), f32),
            vmem((BLOCK * samples, lanes), f32),
            vmem((samples, 2 * channels, lanes), bf16),
            vmem(((FINE_MAX + 1) * groups, 2 * channels), bf16),
            vmem((groups, channels), i32),
            vmem((bands, trials), i32),
            vmem((bands * trials // LANES, LANES), i32),
            vmem((bands * 16, trials // LANES, LANES), i32),
            vmem((groups * (samples - FINE_MAX), lanes), f32),
            vmem((lanes * trials // LANES, LANES), f32),
            vmem((bands * 16, LANES), f32),
            dma((parts * 4,)),
            dma((2,)),
            dma((parts * 2,)),
            dma((parts * 2,)),
            dma((parts,)),
            dma((parts,)),
            dma((bands,)),
            dma((bands,)),
            pltpu.SemaphoreType.REGULAR((8,)),
        ],
        compiler_params=pltpu.CompilerParams(
            collective_id=0, has_side_effects=True, vmem_limit_bytes=60 * 1024 * 1024
        ),
        cost_estimate=pl.CostEstimate(flops=10**9, bytes_accessed=11 * 10**6, transcendentals=0),
    )(voltages, fine_delays, coarse_delays.T)


def solution(mesh):
    in_specs = (P("feed", None, "chan", None, None), P(), P())
    out_specs = P(None, ("feed", "chan"), None)
    return jax.shard_map(local, mesh=mesh, in_specs=in_specs, out_specs=out_specs, check_vma=False)
```

```python
import functools
import math

import jax
import jax.numpy as jnp
from jax import lax
from jax.experimental import pallas as pl
from jax.experimental.pallas import tpu as pltpu
from jax.sharding import PartitionSpec as P

FINE_MAX = 8
COARSE_MAX = 16
NWID = 4
MESH = pl.DeviceIdType.MESH

epsilon = 1e-06
PART = 8
BLOCK = 16
LANES = 128
AHEAD = 4


def gather_lanes(x, index):
    numbers = lax.GatherDimensionNumbers(
        offset_dims=(),
        collapsed_slice_dims=(1,),
        start_index_map=(1,),
        operand_batching_dims=(0,),
        start_indices_batching_dims=(0,),
    )
    return lax.gather(
        x, index[..., None], numbers, (1, 1), mode=lax.GatherScatterMode.PROMISE_IN_BOUNDS
    )


def kernel(
    bands, total_channels,
    v_hbm, fine_hbm, coarse_hbm, out_ref,
    v, s1, r1, zs, r2, xt, xhl, mask, fd, cd, cdt, idx, o, m, r3,
    load_sem, side_sem, d_send, d_recv, z_send, z_recv, a_send, a_recv, met_sem,
):
    parts = v.shape[1]
    samples = v.shape[4]
    lanes = v.shape[5]
    rows = PART * samples
    packed = rows // 2
    groups = fd.shape[0]
    width = fd.shape[1]
    span = samples - FINE_MAX
    rowsets = cd.shape[1] // LANES
    feed = lax.axis_index("feed")
    me = lax.axis_index("chan")
    core, low = lax.rem(feed, 2), lax.div(feed, 2)

    def quarter(r):
        return lax.rem(low + r // 2, 2) * 2 + lax.rem(core + r % 2, 2)

    core_peer, chip_peer = quarter(1), quarter(2)

    def load(i, r):
        return pltpu.make_async_copy(
            v_hbm.at[0, :, pl.ds(i * PART, PART), :, pl.ds(pl.multiple_of(quarter(r) * lanes, lanes), lanes)],
            v.at[r, i],
            load_sem.at[i * 4 + r],
        )

    def to_core(i, p):
        return pltpu.make_async_remote_copy(
            src_ref=s1.at[i, p], dst_ref=r1.at[i, p],
            send_sem=d_send.at[i * 2 + p], recv_sem=d_recv.at[i * 2 + p],
            device_id=(core_peer, me), device_id_type=MESH,
        )

    def to_chip(h, i):
        return pltpu.make_async_remote_copy(
            src_ref=zs.at[h, i], dst_ref=r2.at[h, i],
            send_sem=z_send.at[h * parts + i], recv_sem=z_recv.at[h * parts + i],
            device_id=(chip_peer, me), device_id_type=MESH,
        )

    spot, plane = lax.rem(me, 4), lax.div(me, 4)
    planes = bands // 4
    way = 2 * low - 1

    def wrap(x):
        return lax.rem(x + 16, 4)

    def goal(h, n):
        which = lax.rem(n, 2)
        k = lax.rem(plane + lax.div(n, 2), planes) * 4 + wrap(spot + (h + which) * way)
        return k, lax.rem(low + which, 2) * 2 + core

    def origin(h, n):
        which = lax.rem(n, 2)
        return lax.rem(plane + planes - lax.div(n, 2), planes) * 4 + wrap(
            spot - (h + which) * way * (1 - 2 * which)
        )

    def block(k):
        return pl.ds(pl.multiple_of(k * 16, 16), 16)

    def to_band(h, n, slot):
        k, owner = goal(h, n)
        return pltpu.make_async_remote_copy(
            src_ref=m.at[h, block(k)], dst_ref=r3.at[block(slot)],
            send_sem=a_send.at[h * (bands // 2) + n], recv_sem=a_recv.at[slot],
            device_id=(owner, k), device_id_type=MESH,
        )

    def fetch(i):
        for r in (3, 1, 2, 0):
            load(i, r).start()

    fetch(0)

    barrier = pltpu.get_barrier_semaphore()
    pl.semaphore_signal(barrier, inc=1, device_id=(core_peer, me), device_id_type=MESH)
    pl.semaphore_signal(barrier, inc=1, device_id=(chip_peer, me), device_id_type=MESH)

    ring = min(bands, 4)
    digit = lax.rem(me, ring)
    friends = [[me - digit + lax.rem(digit + 1, ring)]]
    if ring > 2:
        friends[0].append(me - digit + lax.rem(digit + ring - 1, ring))
    bit = ring
    while bit < bands:
        friends.append([me + (1 - 2 * lax.rem(lax.div(me, bit), 2)) * bit])
        bit *= 2
    for turn in friends:
        for k in turn:
            pl.semaphore_signal(barrier, inc=1, device_id=(feed, k), device_id_type=MESH)
    for i in range(1, AHEAD):
        fetch(i)
    own_fine = pltpu.make_async_copy(
        fine_hbm.at[:, pl.ds(pl.multiple_of(me * width, width), width)], fd, side_sem.at[0]
    )
    own_fine.start()
    all_coarse = pltpu.make_async_copy(coarse_hbm, cd, side_sem.at[1])
    all_coarse.start()

    def widen(i, r, p):
        load(i, r).wait()
        s1[i, p] = v[r, i].astype(jnp.float32).reshape(2, rows, lanes)

    where = lax.broadcasted_iota(jnp.int32, (packed, lanes), 1)
    slot = lax.div(lax.rem(where, 8), 2)

    def turned(x):
        at = lax.rem(lax.broadcasted_iota(jnp.int32, x.shape, 1), 8)
        return jnp.where(at < 4, pltpu.roll(x, lanes - 4, 1), pltpu.roll(x, 4, 1))

    def pack(near, far, h, step):
        here = slot == wrap(spot + h * step)
        also = slot == wrap(spot + (h + 1) * step)
        first = jnp.where(here, near[:packed], far[:packed])
        second = jnp.where(here, near[packed:], far[packed:])
        return jnp.where(jnp.logical_or(here, also), first, turned(second))

    def pass_on(i):
        for r in (2, 0):
            load(i, r).wait()
        for p in (1, 0):
            to_core(i, p).wait_recv()
        for c in range(2):
            own = r1[i, 0, c] + v[0, i, c].astype(jnp.float32).reshape(rows, lanes)
            other = r1[i, 1, c] + v[2, i, c].astype(jnp.float32).reshape(rows, lanes)
            for h in range(2):
                zs[h, i, c] = pack(other, own, h, -way)
                r1[i, 0, c, h * packed : (h + 1) * packed, :] = pack(own, other, h, way)
        to_chip(0, i).start()

    widen(0, 3, 1)
    widen(0, 1, 0)
    pl.semaphore_wait(barrier, 2 + sum(len(turn) for turn in friends))
    to_core(0, 1).start()
    to_core(0, 0).start()

    @pl.loop(1, parts)
    def _(i):
        @pl.when(i + AHEAD - 1 < parts)
        def _():
            fetch(i + AHEAD - 1)

        for r, p in ((3, 1), (1, 0)):
            widen(i, r, p)
            to_core(i, p).start()
        pass_on(i - 1)

    pass_on(parts - 1)

    for turn, ks in enumerate(friends):
        if turn or ring > 2:
            for k in ks:
                pl.semaphore_signal(
                    met_sem.at[turn], inc=1, device_id=(feed, k), device_id_type=MESH
                )
            pl.semaphore_wait(met_sem.at[turn], len(ks))

    pl.semaphore_signal(
        met_sem.at[len(friends)], inc=1, device_id=(chip_peer, me), device_id_type=MESH
    )
    pl.semaphore_wait(met_sem.at[len(friends)], 1)

    own_fine.wait()
    place_of = lax.broadcasted_iota(jnp.int32, (8, width), 1)
    in_four = lax.rem(lax.div(place_of, 4), 4)
    order = place_of + jnp.where(in_four == 1, 4, 0) - jnp.where(in_four == 2, 4, 0)
    delays = jnp.concatenate(
        [gather_lanes(fd[q : q + 8, :], order) for q in range(0, groups, 8)], axis=0
    )
    for delay in range(FINE_MAX + 1):
        chosen = jnp.where(delays == delay, 1.0, 0.0).astype(jnp.bfloat16)
        mask[delay * groups : (delay + 1) * groups, :width] = chosen
        mask[delay * groups : (delay + 1) * groups, width:] = chosen

    all_coarse.wait()
    for q in range(rowsets):
        cdt[pl.ds(q, bands, stride=rowsets), :] = cd[:, q * LANES : (q + 1) * LANES]
    lane = lax.broadcasted_iota(jnp.int32, (rowsets, LANES), 1)
    base = lane - lax.rem(lane, span) + lax.rem(lane, 16)
    first = lane - lax.rem(lane, 16)

    @pl.loop(0, bands)
    def _(s):
        codes = cdt[pl.ds(pl.multiple_of(s * rowsets, rowsets), rowsets), :]
        for j in range(16):
            idx[s * 16 + j] = base + gather_lanes(codes, first + j)

    def normalise(h, i, place):
        to_chip(h, i).wait_recv()
        power = None
        for c in range(2):
            half = pl.ds(pl.multiple_of(h * packed, 8), packed)
            total = r1[i, 0, c, half, :] + r2[h, i, c]
            power = total * total if power is None else power + total * total
        power = power.reshape(PART // 2, samples, lanes)
        level = jnp.sum(power, axis=1, keepdims=True) * (1.0 / samples)
        value = power * (1.0 / (level + epsilon)) - 1.0
        xt[place * packed : (place + 1) * packed, :] = value.reshape(packed, lanes)

    each = BLOCK // PART
    blocks = parts // each

    def prepare(h, g):
        for place in range(each):
            normalise(h, g * each + place, place)
        for t in range(samples):
            value = xt[pl.ds(t, BLOCK // 2, stride=samples), :]
            value = jnp.concatenate([value, turned(value)], axis=0)
            high = value.astype(jnp.bfloat16)
            low_part = (value - high.astype(jnp.float32)).astype(jnp.bfloat16)
            xhl[t, pl.ds(pl.multiple_of(g * BLOCK, BLOCK), BLOCK), :] = high
            xhl[t, pl.ds(pl.multiple_of(width + g * BLOCK, BLOCK), BLOCK), :] = low_part

    def release(g):
        for place in range(each):
            to_chip(1, g * each + place).start()

    @pl.loop(0, blocks)
    def _(g):
        @pl.when(g == blocks - 2)
        def _():
            release(0)

        prepare(0, g)

    release(1)

    @pl.loop(0, parts)
    def _(i):
        to_core(i, 0).wait_send()
        to_core(i, 1).wait_send()

    terms = (FINE_MAX + 1) * groups

    def finish(h):
        for i in range(samples // 4):
            for p in range(2):
                both = jnp.concatenate([xhl[i * 4 + p * 2], xhl[i * 4 + p * 2 + 1]], axis=1)
                product = jnp.dot(mask[...], both, preferred_element_type=jnp.float32)
                s1[i, p, 0, :terms, :] = product[:, :lanes]
                s1[i, p, 1, :terms, :] = product[:, lanes:]

        for t in range(span):
            total = None
            for delay in range(FINE_MAX + 1):
                at = t + delay
                term = s1[at // 4, at // 2 % 2, at % 2, delay * groups : (delay + 1) * groups, :]
                total = term if total is None else total + term
            o[pl.ds(t, groups, stride=span), :] = total

        for q in range(rowsets):
            m[h, pl.ds(q, lanes, stride=rowsets), :] = o[q * LANES : (q + 1) * LANES, :].T

        @pl.loop(1 - h, bands // 2)
        def _(n):
            to_band(h, n, me).start()

    finish(0)
    r3[block(me), :] = m[0, block(me), :]

    @pl.loop(0, blocks - 2)
    def _(g):
        release(g + 2)
        prepare(1, g)

    def collect(s, totals):
        totals = list(totals)
        pair = [
            r3[pl.ds(pl.multiple_of(s * 16 + b * rowsets, rowsets), rowsets), :] for b in range(2)
        ]
        for j in range(16):
            index = idx[s * 16 + j]
            for b in range(2):
                totals[b * 16 + j] = totals[b * 16 + j] + gather_lanes(pair[b], index)
        return tuple(totals)

    together = min(8, bands // 2)

    def step(h, turn, totals):
        sources = []
        for n in range(together):
            n += turn * together
            s = origin(h, n)
            sources.append(s)
            if h == 0:

                @pl.when(n > 0)
                def _():
                    to_band(h, n, s).wait()
            else:
                to_band(h, n, s).wait()
        for s in sources:
            totals = collect(s, totals)
        return totals

    totals = (jnp.zeros((rowsets, LANES), jnp.float32),) * 32
    turns = bands // 2 // together
    totals = lax.fori_loop(0, turns, functools.partial(step, 0), totals)
    for g in range(blocks - 2, blocks):
        prepare(1, g)
    finish(1)

    @pl.loop(0, 2 * parts)
    def _(i):
        to_chip(lax.div(i, parts), lax.rem(i, parts)).wait_send()

    totals = lax.fori_loop(0, turns, functools.partial(step, 1), totals)

    box = jnp.concatenate([totals[b * 16 + j] for j in range(16) for b in range(2)], axis=0)

    def sample_of(x):
        return lax.rem(lax.broadcasted_iota(jnp.int32, x.shape, 1), 16)

    def ahead(x, n):
        return pltpu.roll(x, LANES - n, 1)

    for k in range(NWID):
        best = jnp.where(sample_of(box) <= 16 - 2**k, box, -jnp.inf)
        for n in (8, 4, 2, 1):
            half = best.shape[0] // 2
            a, b = best[:half], best[half:]
            upper = lax.rem(lax.div(sample_of(a), n), 2) == 1
            best = jnp.maximum(
                jnp.where(upper, pltpu.roll(b, n, 1), a), jnp.where(upper, b, ahead(a, n))
            )
        result = best * (1.0 / math.sqrt(2**k * total_channels))
        for b in range(2):
            for q in range(rowsets):
                row = b * rowsets + q
                out_ref[k, b : b + 1, q * LANES : (q + 1) * LANES] = result[row : row + 1, :]
        if k + 1 < NWID:
            box = box + ahead(box, 2**k)


def local(voltages, fine_delays, coarse_delays):
    _, _, channels, samples, beams = voltages.shape
    groups, total_channels = fine_delays.shape
    trials, bands = coarse_delays.shape
    lanes = beams // lax.axis_size("feed")
    parts = channels // PART
    rows = PART * samples
    f32, bf16, i32 = jnp.float32, jnp.bfloat16, jnp.int32
    dma = pltpu.SemaphoreType.DMA
    vmem = pltpu.VMEM
    return pl.pallas_call(
        functools.partial(kernel, bands, total_channels),
        out_shape=jax.ShapeDtypeStruct((NWID, beams // (lax.axis_size("feed") * bands), trials), f32),
        in_specs=[pl.BlockSpec(memory_space=pl.ANY)] * 3,
        out_specs=pl.BlockSpec(memory_space=pltpu.VMEM),
        scratch_shapes=[
            vmem((4, parts, 2, PART, samples, lanes), bf16),
            vmem((parts, 2, 2, rows, lanes), f32),
            vmem((parts, 2, 2, rows, lanes), f32),
            vmem((2, parts, 2, rows // 2, lanes), f32),
            vmem((2, parts, 2, rows // 2, lanes), f32),
            vmem((BLOCK // 2 * samples, lanes), f32),
            vmem((samples, 2 * channels, lanes), bf16),
            vmem(((FINE_MAX + 1) * groups, 2 * channels), bf16),
            vmem((groups, channels), i32),
            vmem((bands, trials), i32),
            vmem((bands * trials // LANES, LANES), i32),
            vmem((bands * 16, trials // LANES, LANES), i32),
            vmem((groups * (samples - FINE_MAX), lanes), f32),
            vmem((2, lanes * trials // LANES, LANES), f32),
            vmem((bands * 16, LANES), f32),
            dma((parts * 4,)),
            dma((2,)),
            dma((parts * 2,)),
            dma((parts * 2,)),
            dma((2 * parts,)),
            dma((2 * parts,)),
            dma((bands,)),
            dma((bands,)),
            pltpu.SemaphoreType.REGULAR((8,)),
        ],
        compiler_params=pltpu.CompilerParams(
            collective_id=0, has_side_effects=True, vmem_limit_bytes=60 * 1024 * 1024
        ),
        cost_estimate=pl.CostEstimate(flops=10**9, bytes_accessed=11 * 10**6, transcendentals=0),
    )(voltages, fine_delays, coarse_delays.T)


def solution(mesh):
    in_specs = (P("feed", None, "chan", None, None), P(), P())
    out_specs = P(None, ("feed", "chan"), None)
    return jax.shard_map(local, mesh=mesh, in_specs=in_specs, out_specs=out_specs, check_vma=False)
```

```python
import functools
import math

import jax
import jax.numpy as jnp
from jax import lax
from jax.experimental import pallas as pl
from jax.experimental.pallas import tpu as pltpu
from jax.sharding import PartitionSpec as P

FINE_MAX = 8
COARSE_MAX = 16
NWID = 4
MESH = pl.DeviceIdType.MESH

epsilon = 1e-06
PART = 8
BLOCK = 16
LANES = 128
AHEAD = 4


def gather_lanes(x, index):
    numbers = lax.GatherDimensionNumbers(
        offset_dims=(),
        collapsed_slice_dims=(1,),
        start_index_map=(1,),
        operand_batching_dims=(0,),
        start_indices_batching_dims=(0,),
    )
    return lax.gather(
        x, index[..., None], numbers, (1, 1), mode=lax.GatherScatterMode.PROMISE_IN_BOUNDS
    )


def kernel(
    bands, total_channels,
    v_hbm, fine_hbm, coarse_hbm, out_ref,
    v, s1, r1, zs, r2, xt, xhl, mask, fd, cd, cdt, idx, o, m, r3,
    load_sem, side_sem, d_send, d_recv, z_send, z_recv, a_send, a_recv, met_sem,
):
    parts = v.shape[1]
    samples = v.shape[4]
    lanes = v.shape[5]
    rows = PART * samples
    packed = rows // 2
    groups = fd.shape[0]
    width = fd.shape[1]
    span = samples - FINE_MAX
    rowsets = cd.shape[1] // LANES
    feed = lax.axis_index("feed")
    me = lax.axis_index("chan")
    core, low = lax.rem(feed, 2), lax.div(feed, 2)

    def quarter(r):
        return lax.rem(low + r // 2, 2) * 2 + lax.rem(core + r % 2, 2)

    core_peer, chip_peer = quarter(1), quarter(2)

    def load(i, r):
        return pltpu.make_async_copy(
            v_hbm.at[0, :, pl.ds(i * PART, PART), :, pl.ds(pl.multiple_of(quarter(r) * lanes, lanes), lanes)],
            v.at[r, i],
            load_sem.at[i * 4 + r],
        )

    def to_core(i, p):
        return pltpu.make_async_remote_copy(
            src_ref=s1.at[i, p], dst_ref=r1.at[i, p],
            send_sem=d_send.at[i * 2 + p], recv_sem=d_recv.at[i * 2 + p],
            device_id=(core_peer, me), device_id_type=MESH,
        )

    def to_chip(h, i):
        return pltpu.make_async_remote_copy(
            src_ref=zs.at[h, i], dst_ref=r2.at[h, i],
            send_sem=z_send.at[h * parts + i], recv_sem=z_recv.at[h * parts + i],
            device_id=(chip_peer, me), device_id_type=MESH,
        )

    spot, plane = lax.rem(me, 4), lax.div(me, 4)
    planes = bands // 4
    way = 2 * low - 1

    def wrap(x):
        return lax.rem(x + 16, 4)

    def goal(h, n):
        which = lax.rem(n, 2)
        k = lax.rem(plane + lax.div(n, 2), planes) * 4 + wrap(spot + (h + which) * way)
        return k, lax.rem(low + which, 2) * 2 + core

    def origin(h, n):
        which = lax.rem(n, 2)
        return lax.rem(plane + planes - lax.div(n, 2), planes) * 4 + wrap(
            spot - (h + which) * way * (1 - 2 * which)
        )

    def block(k):
        return pl.ds(pl.multiple_of(k * 16, 16), 16)

    def to_band(h, n, slot):
        k, owner = goal(h, n)
        return pltpu.make_async_remote_copy(
            src_ref=m.at[h, block(k)], dst_ref=r3.at[block(slot)],
            send_sem=a_send.at[h * (bands // 2) + n], recv_sem=a_recv.at[slot],
            device_id=(owner, k), device_id_type=MESH,
        )

    def fetch(i):
        for r in (3, 1, 2, 0):
            load(i, r).start()

    fetch(0)

    barrier = pltpu.get_barrier_semaphore()
    pl.semaphore_signal(barrier, inc=1, device_id=(core_peer, me), device_id_type=MESH)
    pl.semaphore_signal(barrier, inc=1, device_id=(chip_peer, me), device_id_type=MESH)

    ring = min(bands, 4)
    digit = lax.rem(me, ring)
    friends = [[me - digit + lax.rem(digit + 1, ring)]]
    if ring > 2:
        friends[0].append(me - digit + lax.rem(digit + ring - 1, ring))
    bit = ring
    while bit < bands:
        friends.append([me + (1 - 2 * lax.rem(lax.div(me, bit), 2)) * bit])
        bit *= 2
    for turn in friends:
        for k in turn:
            pl.semaphore_signal(barrier, inc=1, device_id=(feed, k), device_id_type=MESH)
    for i in range(1, AHEAD):
        fetch(i)
    own_fine = pltpu.make_async_copy(
        fine_hbm.at[:, pl.ds(pl.multiple_of(me * width, width), width)], fd, side_sem.at[0]
    )
    own_fine.start()
    all_coarse = pltpu.make_async_copy(coarse_hbm, cd, side_sem.at[1])
    all_coarse.start()

    def widen(i, r, p):
        load(i, r).wait()
        s1[i, p] = v[r, i].astype(jnp.float32).reshape(2, rows, lanes)

    where = lax.broadcasted_iota(jnp.int32, (packed, lanes), 1)
    slot = lax.div(lax.rem(where, 8), 2)

    def turned(x):
        at = lax.rem(lax.broadcasted_iota(jnp.int32, x.shape, 1), 8)
        return jnp.where(at < 4, pltpu.roll(x, lanes - 4, 1), pltpu.roll(x, 4, 1))

    def kept(h, count):
        at = lax.div(lax.rem(lax.broadcasted_iota(jnp.int32, (count, lanes), 1), 8), 2)
        return jnp.logical_or(at == wrap(spot + h * way), at == wrap(spot + (h + 1) * way))

    def pack(near, far, h, step):
        here = slot == wrap(spot + h * step)
        also = slot == wrap(spot + (h + 1) * step)
        first = jnp.where(here, near[:packed], far[:packed])
        second = jnp.where(here, near[packed:], far[packed:])
        return jnp.where(jnp.logical_or(here, also), first, turned(second))

    def pass_on(i):
        for r in (2, 0):
            load(i, r).wait()
        for p in (1, 0):
            to_core(i, p).wait_recv()
        def sums(c):
            return [
                r1[i, p, c] + v[2 * p, i, c].astype(jnp.float32).reshape(rows, lanes)
                for p in range(2)
            ]

        for c in range(2):
            own, other = sums(c)
            zs[0, i, c] = pack(other, own, 0, -way)
        to_chip(0, i).start()
        for c in range(2):
            own, other = sums(c)
            zs[1, i, c] = pack(other, own, 1, -way)
            for h in range(2):
                r1[i, 0, c, h * packed : (h + 1) * packed, :] = pack(own, other, h, way)

    widen(0, 3, 1)
    widen(0, 1, 0)
    pl.semaphore_wait(barrier, 2 + sum(len(turn) for turn in friends))
    to_core(0, 1).start()
    to_core(0, 0).start()
    pass_on(0)

    @pl.loop(1, parts)
    def _(i):
        @pl.when(i + AHEAD - 1 < parts)
        def _():
            fetch(i + AHEAD - 1)

        for r, p in ((3, 1), (1, 0)):
            widen(i, r, p)
            to_core(i, p).start()
        pass_on(i)

    for turn, ks in enumerate(friends):
        if turn or ring > 2:
            for k in ks:
                pl.semaphore_signal(
                    met_sem.at[turn], inc=1, device_id=(feed, k), device_id_type=MESH
                )
            pl.semaphore_wait(met_sem.at[turn], len(ks))

    pl.semaphore_signal(
        met_sem.at[len(friends)], inc=1, device_id=(chip_peer, me), device_id_type=MESH
    )
    pl.semaphore_wait(met_sem.at[len(friends)], 1)

    own_fine.wait()
    place_of = lax.broadcasted_iota(jnp.int32, (8, width), 1)
    in_four = lax.rem(lax.div(place_of, 4), 4)
    order = place_of + jnp.where(in_four == 1, 4, 0) - jnp.where(in_four == 2, 4, 0)
    delays = jnp.concatenate(
        [gather_lanes(fd[q : q + 8, :], order) for q in range(0, groups, 8)], axis=0
    )
    for delay in range(FINE_MAX + 1):
        chosen = jnp.where(delays == delay, 1.0, 0.0).astype(jnp.bfloat16)
        mask[delay * groups : (delay + 1) * groups, :width] = chosen
        mask[delay * groups : (delay + 1) * groups, width:] = chosen

    all_coarse.wait()
    for q in range(rowsets):
        cdt[pl.ds(q, bands, stride=rowsets), :] = cd[:, q * LANES : (q + 1) * LANES]
    lane = lax.broadcasted_iota(jnp.int32, (rowsets, LANES), 1)
    base = lane - lax.rem(lane, span) + lax.rem(lane, 16)
    first = lane - lax.rem(lane, 16)

    @pl.loop(0, bands)
    def _(s):
        codes = cdt[pl.ds(pl.multiple_of(s * rowsets, rowsets), rowsets), :]
        for j in range(16):
            idx[s * 16 + j] = base + gather_lanes(codes, first + j)

    def normalise(h, i, place):
        to_chip(h, i).wait_recv()
        power = None
        for c in range(2):
            half = pl.ds(pl.multiple_of(h * packed, 8), packed)
            total = r1[i, 0, c, half, :] + r2[h, i, c]
            power = total * total if power is None else power + total * total
        power = power.reshape(PART // 2, samples, lanes)
        level = jnp.sum(power, axis=1, keepdims=True) * (1.0 / samples)
        value = power * (1.0 / (level + epsilon)) - 1.0
        xt[place * packed : (place + 1) * packed, :] = value.reshape(packed, lanes)

    each = BLOCK // PART
    blocks = parts // each

    def prepare(h, g):
        for place in range(each):
            normalise(h, g * each + place, place)
        keep = kept(h, BLOCK // 2)
        for t in range(samples // 2):
            even = xt[pl.ds(2 * t, BLOCK // 2, stride=samples), :]
            odd = xt[pl.ds(2 * t + 1, BLOCK // 2, stride=samples), :]
            value = jnp.concatenate(
                [jnp.where(keep, even, turned(odd)), jnp.where(keep, turned(even), odd)], axis=0
            )
            high = value.astype(jnp.bfloat16)
            low_part = (value - high.astype(jnp.float32)).astype(jnp.bfloat16)
            xhl[t, pl.ds(pl.multiple_of(g * BLOCK, BLOCK), BLOCK), :] = high
            xhl[t, pl.ds(pl.multiple_of(width + g * BLOCK, BLOCK), BLOCK), :] = low_part

    def release(g):
        for place in range(each):
            to_chip(1, g * each + place).start()

    @pl.loop(0, blocks)
    def _(g):
        @pl.when(g == blocks - 2)
        def _():
            release(0)

        prepare(0, g)

    release(1)

    @pl.loop(0, parts)
    def _(i):
        to_core(i, 0).wait_send()
        to_core(i, 1).wait_send()

    terms = (FINE_MAX + 1) * groups

    def finish(h):
        for i in range(samples // 8):
            for p in range(2):
                both = jnp.concatenate([xhl[i * 4 + p * 2], xhl[i * 4 + p * 2 + 1]], axis=1)
                product = jnp.dot(mask[...], both, preferred_element_type=jnp.float32)
                s1[i, p, 0, :terms, :] = product[:, :lanes]
                s1[i, p, 1, :terms, :] = product[:, lanes:]

        keep = kept(h, groups)

        def term(at, delay):
            rows_of = slice(delay * groups, (delay + 1) * groups)
            return s1[at // 4, at // 2 % 2, at % 2, rows_of, :]

        for t in range(span // 2):
            total = term(t, 0)
            for delay in range(2, FINE_MAX + 1, 2):
                total = total + term(t + delay // 2, delay)
            crossed = None
            for delay in range(1, FINE_MAX + 1, 2):
                at = t + delay // 2
                value = jnp.where(keep, term(at + 1, delay), term(at, delay))
                crossed = value if crossed is None else crossed + value
            total = total + turned(crossed)
            o[pl.ds(2 * t, groups, stride=span), :] = total
            o[pl.ds(2 * t + 1, groups, stride=span), :] = turned(total)

        for q in range(rowsets):
            m[h, pl.ds(q, lanes, stride=rowsets), :] = o[q * LANES : (q + 1) * LANES, :].T

        @pl.loop(1 - h, bands // 2)
        def _(n):
            to_band(h, n, me).start()

    finish(0)
    r3[block(me), :] = m[0, block(me), :]

    @pl.loop(0, blocks - 2)
    def _(g):
        release(g + 2)
        prepare(1, g)

    def collect(s, totals):
        totals = list(totals)
        pair = [
            r3[pl.ds(pl.multiple_of(s * 16 + b * rowsets, rowsets), rowsets), :] for b in range(2)
        ]
        for j in range(16):
            index = idx[s * 16 + j]
            for b in range(2):
                totals[b * 16 + j] = totals[b * 16 + j] + gather_lanes(pair[b], index)
        return tuple(totals)

    together = min(8, bands // 2)

    def step(h, turn, totals):
        sources = []
        for n in range(together):
            n += turn * together
            s = origin(h, n)
            sources.append(s)
            if h == 0:

                @pl.when(n > 0)
                def _():
                    to_band(h, n, s).wait()
            else:
                to_band(h, n, s).wait()
        for s in sources:
            totals = collect(s, totals)
        return totals

    totals = (jnp.zeros((rowsets, LANES), jnp.float32),) * 32
    turns = bands // 2 // together
    totals = lax.fori_loop(0, turns, functools.partial(step, 0), totals)
    for g in range(blocks - 2, blocks):
        prepare(1, g)
    finish(1)

    @pl.loop(0, 2 * parts)
    def _(i):
        to_chip(lax.div(i, parts), lax.rem(i, parts)).wait_send()

    totals = lax.fori_loop(0, turns, functools.partial(step, 1), totals)

    box = jnp.concatenate([totals[b * 16 + j] for j in range(16) for b in range(2)], axis=0)

    def sample_of(x):
        return lax.rem(lax.broadcasted_iota(jnp.int32, x.shape, 1), 16)

    def ahead(x, n):
        return pltpu.roll(x, LANES - n, 1)

    for k in range(NWID):
        best = jnp.where(sample_of(box) <= 16 - 2**k, box, -jnp.inf)
        for n in (8, 4, 2, 1):
            half = best.shape[0] // 2
            a, b = best[:half], best[half:]
            upper = lax.rem(lax.div(sample_of(a), n), 2) == 1
            best = jnp.maximum(
                jnp.where(upper, pltpu.roll(b, n, 1), a), jnp.where(upper, b, ahead(a, n))
            )
        result = best * (1.0 / math.sqrt(2**k * total_channels))
        for b in range(2):
            part = result[b * rowsets : (b + 1) * rowsets]
            out_ref[pl.ds(k * 2 * rowsets + b, rowsets, stride=2), :] = part
        if k + 1 < NWID:
            box = box + ahead(box, 2**k)


def local(voltages, fine_delays, coarse_delays):
    _, _, channels, samples, beams = voltages.shape
    groups, total_channels = fine_delays.shape
    trials, bands = coarse_delays.shape
    lanes = beams // lax.axis_size("feed")
    parts = channels // PART
    rows = PART * samples
    f32, bf16, i32 = jnp.float32, jnp.bfloat16, jnp.int32
    dma = pltpu.SemaphoreType.DMA
    vmem = pltpu.VMEM
    largest = pl.pallas_call(
        functools.partial(kernel, bands, total_channels),
        out_shape=jax.ShapeDtypeStruct((NWID * 2 * trials // LANES, LANES), f32),
        in_specs=[pl.BlockSpec(memory_space=pl.ANY)] * 3,
        out_specs=pl.BlockSpec(memory_space=pltpu.VMEM),
        scratch_shapes=[
            vmem((4, parts, 2, PART, samples, lanes), bf16),
            vmem((parts, 2, 2, rows, lanes), f32),
            vmem((parts, 2, 2, rows, lanes), f32),
            vmem((2, parts, 2, rows // 2, lanes), f32),
            vmem((2, parts, 2, rows // 2, lanes), f32),
            vmem((BLOCK // 2 * samples, lanes), f32),
            vmem((samples // 2, 2 * channels, lanes), bf16),
            vmem(((FINE_MAX + 1) * groups, 2 * channels), bf16),
            vmem((groups, channels), i32),
            vmem((bands, trials), i32),
            vmem((bands * trials // LANES, LANES), i32),
            vmem((bands * 16, trials // LANES, LANES), i32),
            vmem((groups * (samples - FINE_MAX), lanes), f32),
            vmem((2, lanes * trials // LANES, LANES), f32),
            vmem((bands * 16, LANES), f32),
            dma((parts * 4,)),
            dma((2,)),
            dma((parts * 2,)),
            dma((parts * 2,)),
            dma((2 * parts,)),
            dma((2 * parts,)),
            dma((bands,)),
            dma((bands,)),
            pltpu.SemaphoreType.REGULAR((8,)),
        ],
        compiler_params=pltpu.CompilerParams(
            collective_id=0, has_side_effects=True, vmem_limit_bytes=60 * 1024 * 1024
        ),
        cost_estimate=pl.CostEstimate(flops=10**9, bytes_accessed=11 * 10**6, transcendentals=0),
    )(voltages, fine_delays, coarse_delays.T)
    largest = largest.reshape(NWID, trials // LANES, 2, LANES)
    return jnp.transpose(largest, (0, 2, 1, 3)).reshape(NWID, 2, trials)


def solution(mesh):
    in_specs = (P("feed", None, "chan", None, None), P(), P())
    out_specs = P(None, ("feed", "chan"), None)
    return jax.shard_map(local, mesh=mesh, in_specs=in_specs, out_specs=out_specs, check_vma=False)
```
